256 devices in a mesh: dp: 32 (over y, z), tensor: 8 (over x, core).
Axes of the slice: x: 4, y: 4, z: 8, core: 2. Of those that a mesh axis runs over, the one named last changes fastest.
Arguments:
- momentum: bfloat16 [8192, 28672], P('dp', 'tensor'), may hold values from -6 to 6
- grad: bfloat16 [8192, 28672], P('dp', 'tensor'), may hold values from -70 to 70
- basis: float32 [1024, 28672], P('dp', 'tensor'), may hold values from -6 to 6
Outputs:
- update: bfloat16 [8192, 28672], P('dp', 'tensor')
- new_momentum: bfloat16 [8192, 28672], P('dp', 'tensor')
- new_basis: float32 [1024, 28672], P('dp', 'tensor')
The draws below stay inside these ranges and needn't reach their ends.
All inputs are finite; a program needn't handle non-finite values.
Results may differ from the reference program's by a relative error of at most 0.024.
Values may be sent and summed in bfloat16 or wider, within the bound.
No kernel may reach another device: no remote copies, remote signals or barrier semaphores. Data moves between devices by JAX's collectives and lax.ppermute only.
A program may use at most 128 MiB of HBM per device.

```python
import math
import jax
import jax.numpy as jnp
from jax import lax

D = 8192
FF = 28672
R = 1024
N_DP = 32


def draw_grad(key, part):
    key = jax.random.fold_in(key, 7)
    key_rows, key_cols, key_base = jax.random.split(key, 3)
    row_place = jnp.arange(D, dtype=jnp.float32)[:, None] / D
    row_scale = jnp.exp(jax.random.uniform(key_rows, (D, 1), jnp.float32, -1.2, 0.0) + 1.1 * row_place)
    position_ramp = jnp.arange(FF, dtype=jnp.float32)[None, :] / FF
    col_scale = jnp.exp(jax.random.uniform(key_cols, (1, FF), jnp.float32, -1.2, 1.1) + 0.55 * position_ramp - 0.3)
    base_values = jnp.clip(jax.random.normal(key_base, (D, FF), jnp.float32), -6.0, 6.0)
    return (base_values * row_scale * col_scale).astype(jnp.bfloat16)


def block_scale(rng, dims, pieces, smallest, largest):
    loudness = 1.0
    for axis_at, shards_of in pieces:
        steps = jax.random.uniform(jax.random.fold_in(jax.random.fold_in(rng, 6), axis_at), (shards_of,), jnp.float32, smallest / len(pieces), largest / len(pieces))
        loudness = loudness * jnp.repeat(jnp.exp(steps), dims[axis_at] // shards_of).reshape((-1,) + (1,) * (len(dims) - 1 - axis_at))
    return loudness


def scatter_about(rng, extent, scale, limit, shards=(), kind=jnp.bfloat16):
    array = jax.random.normal(rng, extent, jnp.float32) * scale
    if len(shards) > 0:
        array = block_scale(rng, extent, shards, -0.22, 0.18) * array
    return jnp.clip(array, min=-limit, max=limit).astype(kind)


def setup_inputs(seed: int = 0) -> dict:
    arg_keys = jax.random.split(jax.random.key(seed), 4)
    momentum = scatter_about(arg_keys[0], (D, FF), 1.0, 6.0, ((0, 32), (1, 8)))
    grad = draw_grad(jax.random.fold_in(arg_keys[3], 71), 0)
    basis = scatter_about(arg_keys[2], (R, FF), 1.0, 6.0, ((0, 32), (1, 8)), jnp.float32)
    return {"momentum": momentum, "grad": grad, "basis": basis}


MOMENTUM = 0.95
JITTER = 0.001
NORM_EPS = 1e-08

def inverse_factor(gram_matrix):
    order_size = gram_matrix.shape[0]
    identity = jnp.eye(order_size, dtype=jnp.float32)
    shifted = gram_matrix + JITTER * jnp.trace(gram_matrix) / order_size * identity
    lower_factor = jnp.linalg.cholesky(shifted)
    return jax.scipy.linalg.solve_triangular(lower_factor, identity, lower=True)

def reference(momentum, grad, basis):
    summed = (momentum.astype(jnp.float32) + grad.astype(jnp.float32)).astype(jnp.bfloat16)
    summed = lax.optimization_barrier(summed)
    narrow_basis = basis.astype(jnp.bfloat16)
    sketch = lax.dot_general(summed.astype(jnp.float32), narrow_basis.astype(jnp.float32), (((1,), (1,)), ((), ())), preferred_element_type=jnp.float32)
    gram_matrix = jnp.dot(sketch.T.astype(jnp.float32), sketch.astype(jnp.float32), precision=lax.Precision.HIGHEST, preferred_element_type=jnp.float32)
    orthonormal = jnp.dot(sketch.astype(jnp.float32), inverse_factor(gram_matrix).T.astype(jnp.float32), precision=lax.Precision.HIGHEST, preferred_element_type=jnp.float32).astype(jnp.bfloat16)
    block_rows = D // N_DP

    def accumulate(running, block_index):
        start_row = (block_index * block_rows).astype(jnp.int32)
        ortho_rows = lax.dynamic_slice_in_dim(orthonormal, start_row, block_rows, 0)
        summed_rows = lax.dynamic_slice_in_dim(summed, start_row, block_rows, 0)
        partial_value = lax.dot_general(ortho_rows.astype(jnp.float32), summed_rows.astype(jnp.float32), (((0,), (0,)), ((), ())), preferred_element_type=jnp.float32).astype(jnp.bfloat16)
        partial_value = lax.optimization_barrier(partial_value)
        return (running + partial_value.astype(jnp.float32), None)
    coefficients, _ = lax.scan(accumulate, jnp.zeros((R, FF), jnp.float32), jnp.arange(N_DP, dtype=jnp.int32))
    column_norms = jnp.sqrt(lax.optimization_barrier(jnp.sum(coefficients * coefficients, axis=1))) + NORM_EPS
    new_basis = math.sqrt(FF) * coefficients / column_norms[:, None]
    narrow_coefficients = coefficients.astype(jnp.bfloat16)
    scaling = math.sqrt(D * FF / R) / column_norms
    scaled = (orthonormal.astype(jnp.float32) * scaling[None, :]).astype(jnp.bfloat16)
    feedback = jnp.dot(orthonormal.astype(jnp.float32), narrow_coefficients.astype(jnp.float32), preferred_element_type=jnp.float32)
    new_momentum = (summed.astype(jnp.float32) - (1.0 - MOMENTUM) * feedback).astype(jnp.bfloat16)
    update = jnp.dot(scaled.astype(jnp.float32), narrow_coefficients.astype(jnp.float32), preferred_element_type=jnp.float32).astype(jnp.bfloat16)
    return (update, new_momentum, new_basis)
```

```python
import functools
import math

import jax
import jax.numpy as jnp
from jax import lax
from jax.experimental import pallas as pl
from jax.experimental.pallas import tpu as pltpu
from jax.sharding import Mesh, PartitionSpec as P

D = 8192
FF = 28672
R = 1024
MOMENTUM = 0.95
JITTER = 0.001
NORM_EPS = 1e-08

DP = ("y", "z")
TENSOR = ("x", "c")
HIGHEST = lax.Precision.HIGHEST
BLOCK = 128


def dot_tn(a, b):
    return lax.dot_general(
        a, b, (((0,), (0,)), ((), ())), precision=HIGHEST, preferred_element_type=jnp.float32
    )


def dot_nn(a, b):
    return lax.dot_general(
        a, b, (((1,), (0,)), ((), ())), precision=HIGHEST, preferred_element_type=jnp.float32
    )


def spread(row):
    return jnp.broadcast_to(row, (8, BLOCK))


def factor_block(a_ref, x_ref):
    rows = lax.broadcasted_iota(jnp.int32, (8, BLOCK), 0)
    for panel in range(BLOCK // 8):
        top = 8 * panel
        a_rows = a_ref[top : top + 8, :]
        x_rows = x_ref[top : top + 8, :]
        pivots = [spread(a_rows[:, top + c : top + c + 1]) for c in range(8)]
        scale = jnp.ones((8, BLOCK), jnp.float32)
        for c in range(8):
            pivot = spread(pivots[c][c : c + 1, :])
            scale = jnp.where(rows == c, lax.rsqrt(pivot), scale)
            if c < 7:
                factor = jnp.where(rows > c, pivots[c] * (1.0 / pivot), 0.0)
                for later in range(c + 1, 8):
                    pivots[later] = pivots[later] - factor * spread(pivots[later][c : c + 1, :])
                a_rows = a_rows - factor * spread(a_rows[c : c + 1, :])
                x_rows = x_rows - factor * spread(x_rows[c : c + 1, :])
        a_rows = a_rows * scale
        x_rows = x_rows * scale
        x_ref[top : top + 8, :] = x_rows
        if panel < BLOCK // 8 - 1:
            columns = a_rows.T
            a_spread = [spread(a_rows[c : c + 1, :]) for c in range(8)]
            x_spread = [spread(x_rows[c : c + 1, :]) for c in range(8)]
            for tile in range(panel + 1, BLOCK // 8):
                at = 8 * tile
                a_tile = a_ref[at : at + 8, :]
                x_tile = x_ref[at : at + 8, :]
                for c in range(8):
                    factor = spread(columns[at : at + 8, c : c + 1])
                    a_tile = a_tile - factor * a_spread[c]
                    x_tile = x_tile - factor * x_spread[c]
                a_ref[at : at + 8, :] = a_tile
                x_ref[at : at + 8, :] = x_tile


def inverse_factor_kernel(size, gram_ref, out_ref, upper, panel_a, panel_x, a_ref, x_ref, shift_ref):
    blocks = size // BLOCK
    shape = (BLOCK, BLOCK)
    eye = lax.broadcasted_iota(jnp.int32, shape, 0) == lax.broadcasted_iota(jnp.int32, shape, 1)
    diagonal = jnp.zeros(shape, jnp.float32)
    for k in range(blocks):
        at = BLOCK * k
        diagonal = diagonal + jnp.where(eye, gram_ref[at : at + BLOCK, at : at + BLOCK], 0.0)
    trace = jnp.sum(jnp.sum(diagonal, axis=1, keepdims=True), axis=0, keepdims=True)
    shift_ref[...] = jnp.where(eye, jnp.broadcast_to(trace * (JITTER / size), shape), 0.0)
    out_ref[...] = jnp.zeros_like(out_ref)

    def step(k, carry):
        for at in range(0, size, BLOCK):

            @pl.when(k == at // BLOCK)
            def _(at=at):
                if at == 0:
                    panel_a[:, :] = gram_ref[0:BLOCK, :]
                    a_ref[...] = gram_ref[0:BLOCK, 0:BLOCK] + shift_ref[...]
                else:
                    above = upper[0:at, at : at + BLOCK]
                    reduced = gram_ref[at : at + BLOCK, at:] - dot_tn(above, upper[0:at, at:])
                    panel_a[:, at:] = reduced
                    a_ref[...] = reduced[:, :BLOCK] + shift_ref[...]
                    panel_x[:, 0:at] = -dot_tn(above, out_ref[0:at, 0:at])

        x_ref[...] = jnp.where(eye, 1.0, 0.0)
        factor_block(a_ref, x_ref)
        for at in range(0, size, BLOCK):

            @pl.when(k == at // BLOCK)
            def _(at=at):
                own = x_ref[...]
                if at + BLOCK < size:
                    upper[at : at + BLOCK, at + BLOCK :] = dot_nn(own, panel_a[:, at + BLOCK :])
                if at > 0:
                    out_ref[at : at + BLOCK, 0:at] = dot_nn(own, panel_x[:, 0:at])
                out_ref[at : at + BLOCK, at : at + BLOCK] = own

        return carry

    lax.fori_loop(0, blocks, step, 0)


def inverse_factor(gram_matrix):
    size = gram_matrix.shape[0]
    return pl.pallas_call(
        functools.partial(inverse_factor_kernel, size),
        out_shape=jax.ShapeDtypeStruct((size, size), jnp.float32),
        in_specs=[pl.BlockSpec(memory_space=pltpu.VMEM)],
        out_specs=pl.BlockSpec(memory_space=pltpu.VMEM),
        scratch_shapes=[
            pltpu.VMEM((size, size), jnp.float32),
            pltpu.VMEM((BLOCK, size), jnp.float32),
            pltpu.VMEM((BLOCK, size), jnp.float32),
            pltpu.VMEM((BLOCK, BLOCK), jnp.float32),
            pltpu.VMEM((BLOCK, BLOCK), jnp.float32),
            pltpu.VMEM((BLOCK, BLOCK), jnp.float32),
        ],
        compiler_params=pltpu.CompilerParams(vmem_limit_bytes=32 * 2**20),
        cost_estimate=pl.CostEstimate(
            flops=60_000_000_000, bytes_accessed=8 * 2**20, transcendentals=0
        ),
    )(gram_matrix)


def halves_psum(array, axes):
    middle = array.shape[0] // 2
    return jnp.concatenate(lax.psum((array[:middle], array[middle:]), axes), axis=0)


def per_device(momentum, grad, basis):
    summed = (momentum.astype(jnp.float32) + grad.astype(jnp.float32)).astype(jnp.bfloat16)
    summed = lax.optimization_barrier(summed)
    narrow_basis = basis.astype(jnp.bfloat16)
    rank_rows = basis.shape[0]
    full_basis = lax.all_gather(narrow_basis, DP, axis=0, tiled=True)
    partial_sketch = lax.dot_general(
        summed, full_basis, (((1,), (1,)), ((), ())), preferred_element_type=jnp.float32
    )
    sketch = halves_psum(partial_sketch, TENSOR)
    gram_matrix = halves_psum(dot_tn(sketch, sketch), DP)
    inverse = inverse_factor(gram_matrix)
    orthonormal = lax.dot_general(
        sketch,
        inverse,
        (((1,), (1,)), ((), ())),
        precision=HIGHEST,
        preferred_element_type=jnp.float32,
    ).astype(jnp.bfloat16)
    partial_coefficients = lax.dot_general(
        orthonormal, summed, (((0,), (0,)), ((), ())), preferred_element_type=jnp.float32
    ).astype(jnp.bfloat16)
    coefficients = halves_psum(partial_coefficients, DP)
    wide = coefficients.astype(jnp.float32)
    column_norms = jnp.sqrt(lax.psum(jnp.sum(wide * wide, axis=1), TENSOR)) + NORM_EPS
    scaling = math.sqrt(D * FF / R) / column_norms
    scaled = (orthonormal.astype(jnp.float32) * scaling[None, :]).astype(jnp.bfloat16)
    feedback = jnp.dot(orthonormal, coefficients, preferred_element_type=jnp.float32)
    new_momentum = (summed.astype(jnp.float32) - (1.0 - MOMENTUM) * feedback).astype(jnp.bfloat16)
    update = jnp.dot(scaled, coefficients, preferred_element_type=jnp.float32).astype(jnp.bfloat16)
    own_start = lax.axis_index(DP) * rank_rows
    own = lax.dynamic_slice_in_dim(coefficients, own_start, rank_rows, 0).astype(jnp.float32)
    own_norms = lax.dynamic_slice_in_dim(column_norms, own_start, rank_rows, 0)
    new_basis = math.sqrt(FF) * own / own_norms[:, None]
    return (update, new_momentum, new_basis)


def solution(mesh):
    split = Mesh(mesh.devices.reshape(4, 8, 4, 2), ("y", "z", "x", "c"))
    spec = P(DP, TENSOR)
    return jax.shard_map(
        per_device, mesh=split, in_specs=(spec,) * 3, out_specs=(spec,) * 3, check_vma=False
    )
```
